32 devices in a mesh: row: 8 (over y, x, core), col: 4 (over z).
Axes of the slice: x: 2, y: 2, z: 4, core: 2. Of those that a mesh axis runs over, the one named last changes fastest.
Arguments:
- node_features: bfloat16 [8192, 512], P(('col', 'row')), may hold values from -6 to 6
- tile_values: bfloat16 [8, 192, 128, 128], P('row', 'col'), may hold values from -0.15625 to 0.15625
- tile_rows: int32 [8, 192], P('row', 'col'), may hold values from 0 to 7, as said below
- tile_cols: int32 [8, 192], P('row', 'col'), may hold values from 0 to 15, as said below
- tile_count: int32 [8, 4], P('row', 'col'), may hold values from 1 to 48, as said below
- weight: bfloat16 [512, 512], replicated, may hold values from -0.25 to 0.25
- bias: float32 [512], replicated, may hold values from -3 to 3
- cotangent: bfloat16 [8192, 512], P(('row', 'col')), may hold values from -6 to 6
Outputs:
- output: bfloat16 [8192, 512], P(('row', 'col'))
- feature_grad: bfloat16 [8192, 512], P(('col', 'row'))
- weight_grad: float32 [512, 512], replicated
- bias_grad: float32 [512], replicated
The draws below stay inside these ranges and needn't reach their ends.
Inputs may be any that keep to these rules, and one draw needn't show every extreme that they name: `tile_rows`: within one grid block the used slots name distinct tiles; together with tile_cols each slot names one tile of the block. `tile_cols`: within one grid block the used slots name distinct tiles. `tile_count`: some grid block uses all 48 slots.
All inputs are finite; a program needn't handle non-finite values.
Results may differ from the reference program's by a relative error of at most 0.014.
Values may be sent and summed in bfloat16 or wider, within the bound.
A program may use at most 128 MiB of HBM per device.

```python
import jax
import jax.numpy as jnp
from jax import lax

F = 512
TILE = 128
RT = 8
CT = 16
TMAX = 48
NODES = 8192
N_ROW = 8
N_COL = 4


def tile_slots(key):
    block_keys = jax.random.split(jax.random.fold_in(key, 11), N_ROW * N_COL)

    def pick_slots(block_key):
        return jax.random.permutation(block_key, RT * CT)[:TMAX]
    slots = jax.vmap(pick_slots)(block_keys)
    return slots.reshape(N_ROW, N_COL * TMAX).astype(jnp.int32)


def draw_tile_rows(key, part):
    return (tile_slots(key) // CT).astype(jnp.int32)


def draw_tile_cols(key, part):
    return (tile_slots(key) % CT).astype(jnp.int32)


def draw_tile_count(key, part):
    levels = jax.random.randint(jax.random.fold_in(key, 23), (N_ROW * N_COL,), 1, 9)
    busiest = jax.random.randint(jax.random.fold_in(key, 29), (), 0, N_ROW * N_COL)
    levels = jnp.where(jnp.arange(N_ROW * N_COL) == busiest, 8, levels)
    totals = jnp.maximum(1, TMAX * levels * levels // 64)
    return totals.reshape(N_ROW, N_COL).astype(jnp.int32)


def block_scale(stream_key, dims, cuts, low, high):
    def one(dim, blocks):
        draws = jax.random.uniform(jax.random.fold_in(jax.random.fold_in(stream_key, 6), dim), (blocks,), jnp.float32, low / len(cuts), high / len(cuts))
        return jnp.repeat(jnp.exp(draws), dims[dim] // blocks).reshape((-1,) + (1,) * (len(dims) - dim - 1))

    factor_of = one(*cuts[0])
    for cut in cuts[1:]:
        factor_of = factor_of * one(*cut)
    return factor_of


def centred(key, shape, scale, most, cuts=(), kind=jnp.bfloat16):
    result = scale * jax.random.normal(key, shape, jnp.float32)
    if cuts:
        result = result * block_scale(key, shape, cuts, -0.22, 0.18)
    return jnp.clip(result, -most, most).astype(kind)


def setup_inputs(seed: int = 0) -> dict:
    key_list = jax.random.split(jax.random.key(seed), 9)
    node_features = centred(key_list[0], (NODES, F), 1.0, 6.0, ((0, 32),))
    tile_values = centred(key_list[1], (N_ROW, N_COL * TMAX, TILE, TILE), (TILE * N_COL * TMAX // (2 * RT)) ** -0.5, 0.15625, ((0, 8), (1, 4)))
    tile_rows = draw_tile_rows(jax.random.fold_in(key_list[8], 71), 0)
    tile_cols = draw_tile_cols(jax.random.fold_in(key_list[8], 71), 0)
    tile_count = draw_tile_count(jax.random.fold_in(key_list[8], 71), 0)
    weight = centred(key_list[5], (F, F), F ** -0.5, 0.25)
    bias = centred(key_list[6], (F,), 0.5, 3.0, (), jnp.float32)
    cotangent = centred(key_list[7], (NODES, F), 1.0, 6.0, ((0, 32),))
    return {"node_features": node_features, "tile_values": tile_values, "tile_rows": tile_rows, "tile_cols": tile_cols, "tile_count": tile_count, "weight": weight, "bias": bias, "cotangent": cotangent}


def block_matrix(values, row_index, col_index, tile_total):
    in_range = jnp.arange(TMAX) < tile_total
    masked = jnp.where(in_range[:, None, None], values.astype(jnp.float32), jnp.float32(0.0))
    layout = jnp.zeros((RT, CT, TILE, TILE), jnp.float32).at[row_index, col_index].add(masked)
    return layout.transpose(0, 2, 1, 3).reshape(RT * TILE, CT * TILE)

def reference(node_features, tile_values, tile_rows, tile_cols, tile_count, weight, bias, cotangent):
    highest = lax.Precision.HIGHEST
    values_all = tile_values.reshape(N_ROW, N_COL, TMAX, TILE, TILE)
    rows_all = tile_rows.reshape(N_ROW, N_COL, TMAX)
    cols_all = tile_cols.reshape(N_ROW, N_COL, TMAX)
    column_blocks = node_features.astype(jnp.float32).reshape(N_COL, CT * TILE, F)

    def forward_block(row_block):
        running = jnp.zeros((RT * TILE, F), jnp.float32)
        for column in range(N_COL):
            matrix = block_matrix(values_all[row_block, column], rows_all[row_block, column], cols_all[row_block, column], tile_count[row_block, column])
            running = running + jnp.dot(matrix, column_blocks[column], precision=highest)
        return running
    summed = lax.map(forward_block, jnp.arange(N_ROW, dtype=jnp.int32))
    aggregated = summed.reshape(NODES, F).astype(jnp.bfloat16)
    pre_act = jnp.dot(aggregated, weight, preferred_element_type=jnp.float32) + bias
    sigmoid_pre = jax.nn.sigmoid(pre_act)
    output = (pre_act * sigmoid_pre).astype(jnp.bfloat16)
    grad_pre = (cotangent.astype(jnp.float32) * sigmoid_pre * (1.0 + pre_act * (1.0 - sigmoid_pre))).astype(jnp.bfloat16)
    grad_scale = 1.0 / jnp.sqrt(jnp.float32(NODES))
    weight_grad = jnp.dot(aggregated.T, grad_pre, preferred_element_type=jnp.float32) * grad_scale
    bias_grad = lax.optimization_barrier(jnp.sum(grad_pre.astype(jnp.float32), axis=0)) * grad_scale
    grad_rows = jnp.dot(grad_pre, weight.T, preferred_element_type=jnp.float32).astype(jnp.bfloat16)
    row_blocks = grad_rows.astype(jnp.float32).reshape(N_ROW, RT * TILE, F)

    def backward_block(column):
        running = jnp.zeros((CT * TILE, F), jnp.float32)
        for row_block in range(N_ROW):
            matrix = block_matrix(values_all[row_block, column], rows_all[row_block, column], cols_all[row_block, column], tile_count[row_block, column])
            running = running + jnp.dot(matrix.T, row_blocks[row_block], precision=highest)
        return running
    column_sums = lax.map(backward_block, jnp.arange(N_COL, dtype=jnp.int32))
    feature_grad = column_sums.reshape(NODES, F).astype(jnp.bfloat16)
    return (output, feature_grad, weight_grad, bias_grad)
```

```python
import functools
import math

import jax
import jax.numpy as jnp
from jax import lax
from jax.experimental import pallas as pl
from jax.experimental.pallas import tpu as pltpu
from jax.sharding import PartitionSpec as P

MESH = pl.DeviceIdType.MESH
BIAS_ROWS = 16


def layer_kernel(
    n_row, n_col, n_chunk,
    slot_ref, x_ref, tiles_hbm, w_hbm, bias_ref, ct_hbm,
    out_ref, fg_ref, wg_ref, bg_ref,
    tiles, a_blk, at_blk, w_ref, ct_ref, xg, part, part_in, own, agg, gp_ref, gg,
    sib_in, tot_in, wb_out, wb_in, wz, wfin,
    local_sem, xl_sem, xs_sem, xf_sem, xr_sem, ps_sem, pr_sem, gs_sem, gr_sem,
    ss_sem, sr_sem, ts_sem, tr_sem, ws_sem, wr_sem, zs_sem, zr_sem, fs_sem, fr_sem,
):
    f32, bf16 = jnp.float32, jnp.bfloat16
    tile_slots = tiles_hbm.shape[0]
    tile = tiles_hbm.shape[1]
    length, features = x_ref.shape
    width = features // n_chunk
    row_tiles = length * n_col // tile
    col_tiles = length * n_row // tile
    n_chip = n_row // 2
    w_rows = features // n_row

    me_r, me_c = lax.axis_index("row"), lax.axis_index("col")
    chip, core = me_r // 2, me_r % 2
    sib = me_r + 1 - 2 * core

    def rows(i):
        return pl.ds(pl.multiple_of(i * length, length), length)

    def remote(src, dst, send, recv, **where):
        return pltpu.make_async_remote_copy(
            src_ref=src, dst_ref=dst, send_sem=send, recv_sem=recv,
            device_id=where, device_id_type=MESH,
        )

    def other_chip(k):
        return lax.rem(chip + k, n_chip)

    def other_col(k):
        return lax.rem(me_c + k, n_col)

    def other_row(k):
        return lax.rem(me_r + k, n_row)

    tiles_copy = pltpu.make_async_copy(tiles_hbm, tiles.at[pl.ds(0, tile_slots)], local_sem.at[0])
    w_copy = pltpu.make_async_copy(w_hbm, w_ref, local_sem.at[1])
    ct_copy = pltpu.make_async_copy(ct_hbm, ct_ref, local_sem.at[2])
    tiles_copy.start()

    def x_chunk(c):
        return x_ref.at[:, pl.ds(c * width, width)]

    def x_local(c):
        return pltpu.make_async_copy(x_chunk(c), xg.at[c, rows(me_r)], xl_sem.at[c])

    for c in range(n_chunk):
        x_local(c).start()
    w_copy.start()
    ct_copy.start()

    barrier = pltpu.get_barrier_semaphore()
    for k in range(1, n_row):
        pl.semaphore_signal(barrier, inc=1, device_id={"row": other_row(k)}, device_id_type=MESH)
    for k in range(1, n_col):
        pl.semaphore_signal(barrier, inc=1, device_id={"col": other_col(k)}, device_id_type=MESH)
    pl.semaphore_wait(barrier, n_row + n_col - 2)

    def x_send(c, k):
        return remote(x_chunk(c), xg.at[c, rows(me_r)], xs_sem.at[c, k], xr_sem.at[c, me_r],
                      row=2 * other_chip(k) + core)

    def x_sib(c):
        return remote(x_chunk(c), xg.at[c, rows(me_r)], xs_sem.at[c, 0], xr_sem.at[c, me_r], row=sib)

    def x_forward(c, k):
        src = 2 * other_chip(n_chip - k) + core
        block = xg.at[c, rows(src)]
        return remote(block, block, xf_sem.at[c, k - 1], xr_sem.at[c, src], row=sib)

    def x_arrival(c, src):
        block = xg.at[c, rows(src)]
        return remote(block, block, xf_sem.at[c, 0], xr_sem.at[c, src], row=sib)

    for c in range(n_chunk):
        for k in range(1, n_chip):
            x_send(c, k).start()
        x_sib(c).start()

    tiles[tile_slots] = jnp.zeros((tile, tile), bf16)
    tiles_copy.wait()

    def dense_row(i, carry):
        for j in range(col_tiles):
            value = tiles[slot_ref[i * col_tiles + j]]
            a_blk[pl.ds(pl.multiple_of(i * tile, tile), tile), pl.ds(j * tile, tile)] = value
        return carry

    lax.fori_loop(0, row_tiles, dense_row, 0)

    def p_send(c, k):
        dest = other_col(k)
        return remote(part.at[c, rows(dest)], part_in.at[c, me_c], ps_sem.at[c, k - 1],
                      pr_sem.at[c, me_c], col=dest)

    def p_arrival(c, src):
        block = part_in.at[c, src]
        return remote(block, block, ps_sem.at[c, 0], pr_sem.at[c, src], col=src)

    for c in range(n_chunk):
        x_local(c).wait()
        for k in range(1, n_chip):
            x_arrival(c, 2 * other_chip(n_chip - k) + core).wait_recv()
            x_forward(c, k).start()
        x_arrival(c, sib).wait_recv()
        for k in range(1, n_chip):
            x_arrival(c, 2 * other_chip(n_chip - k) + 1 - core).wait_recv()

        def forward_block(k, carry):
            dest = other_col(k)
            part[c, rows(dest), :] = jnp.dot(
                a_blk[rows(dest), :], xg[c], preferred_element_type=f32).astype(bf16)
            p_send(c, k).start()
            return carry

        lax.fori_loop(1, n_col, forward_block, 0)
        own[c] = jnp.dot(a_blk[rows(me_c), :], xg[c], preferred_element_type=f32)

    def dense_col(j, carry):
        for i in range(row_tiles):
            value = tiles[slot_ref[i * col_tiles + j]]
            at_blk[pl.ds(pl.multiple_of(j * tile, tile), tile), pl.ds(i * tile, tile)] = value.T
        return carry

    lax.fori_loop(0, col_tiles, dense_col, 0)

    w_copy.wait()
    ct_copy.wait()
    for c in range(n_chunk):
        total = own[c]
        for k in range(1, n_col):
            src = other_col(k)
            p_arrival(c, src).wait_recv()
            total = total + part_in[c, src].astype(f32)
        agg[:, pl.ds(c * width, width)] = total.astype(bf16)

    pre = jnp.dot(agg[...], w_ref[...], preferred_element_type=f32) + bias_ref[...]
    sig = jax.nn.sigmoid(pre)
    grad_pre = (ct_ref[...].astype(f32) * sig * (1.0 + pre * (1.0 - sig))).astype(bf16)
    gp_ref[...] = grad_pre
    out_ref[...] = (pre * sig).astype(bf16)

    def g_send(c, k):
        block = gg.at[c, rows(me_c)]
        return remote(block, block, gs_sem.at[c, k - 1], gr_sem.at[c, me_c], col=other_col(k))

    def g_arrival(c, src):
        block = gg.at[c, rows(src)]
        return remote(block, block, gs_sem.at[c, 0], gr_sem.at[c, src], col=src)

    for c in range(n_chunk):
        gg[c, rows(me_c), :] = lax.dot_general(
            gp_ref[...], w_ref[pl.ds(c * width, width), :], (((1,), (1,)), ((), ())),
            preferred_element_type=f32).astype(bf16)
        for k in range(1, n_col):
            g_send(c, k).start()

    bias_sum = jnp.sum(gp_ref[...].astype(f32), axis=0, keepdims=True)

    def bias_rows(value):
        high = value.astype(bf16).astype(f32)
        low = value - high
        index = lax.broadcasted_iota(jnp.int32, (BIAS_ROWS, features), 0)
        block = jnp.where(index == 0, high, jnp.where(index == 1, low, 0.0))
        return block.astype(bf16)

    bias_block = bias_rows(bias_sum)
    w_local = lax.dot_general(agg[...], gp_ref[...], (((0,), (0,)), ((), ())),
                              preferred_element_type=f32)
    for r in range(n_row):
        wb_out[r, pl.ds(0, w_rows)] = w_local[r * w_rows:(r + 1) * w_rows].astype(bf16)
        wb_out[r, pl.ds(w_rows, BIAS_ROWS)] = bias_block

    def w_send(k):
        dest = other_row(k)
        return remote(wb_out.at[dest], wb_in.at[me_r], ws_sem.at[k - 1], wr_sem.at[me_r], row=dest)

    def w_arrival(src):
        return remote(wb_in.at[src], wb_in.at[src], ws_sem.at[0], wr_sem.at[src], row=src)

    for k in range(1, n_row):
        w_send(k).start()
    wb_in[me_r] = wb_out[me_r]
    for k in range(1, n_row):
        w_arrival(other_row(k)).wait_recv()

    def add_up(ref, count):
        total = ref[0].astype(f32)
        for i in range(1, count):
            total = total + ref[i].astype(f32)
        return total[:w_rows], total[w_rows:w_rows + 1] + total[w_rows + 1:w_rows + 2]

    w_sum, b_sum = add_up(wb_in, n_row)
    wz[me_c, pl.ds(0, w_rows)] = w_sum.astype(bf16)
    wz[me_c, pl.ds(w_rows, BIAS_ROWS)] = bias_rows(b_sum)

    def z_send(k):
        return remote(wz.at[me_c], wz.at[me_c], zs_sem.at[k - 1], zr_sem.at[me_c], col=other_col(k))

    def z_arrival(src):
        return remote(wz.at[src], wz.at[src], zs_sem.at[0], zr_sem.at[src], col=src)

    for k in range(1, n_col):
        z_send(k).start()

    def s_send(c, i):
        return remote(xg.at[c, rows(i)], sib_in.at[c, i], ss_sem.at[c, i], sr_sem.at[c, i], row=sib)

    def t_send(c, k):
        dest = other_chip(k)
        return remote(xg.at[c, rows(n_chip + dest)], tot_in.at[c, chip], ts_sem.at[c, k - 1],
                      tr_sem.at[c, chip], row=2 * dest + core)

    def t_arrival(c, src):
        block = tot_in.at[c, src]
        return remote(block, block, ts_sem.at[c, 0], tr_sem.at[c, src], row=2 * src + core)

    def f_send(k):
        block = wfin.at[me_r]
        return remote(block, block, fs_sem.at[k - 1], fr_sem.at[me_r], row=other_row(k))

    def f_arrival(src):
        return remote(wfin.at[src], wfin.at[src], fs_sem.at[0], fr_sem.at[src], row=src)

    for c in range(n_chunk):
        for k in range(1, n_chip):
            x_forward(c, k).wait_send()

    for c in range(n_chunk):
        for k in range(1, n_col):
            g_arrival(c, other_col(k)).wait_recv()

        def sibling_block(k, carry):
            i = other_chip(k)
            xg[c, rows(i), :] = jnp.dot(at_blk[rows(2 * i + 1 - core), :], gg[c],
                                    preferred_element_type=f32).astype(bf16)
            s_send(c, i).start()
            return carry

        lax.fori_loop(1, n_chip + 1, sibling_block, 0)

        def chip_block(k, carry):
            i = other_chip(k)
            value = jnp.dot(at_blk[rows(2 * i + core), :], gg[c], preferred_element_type=f32)
            s_send(c, i).wait_recv()
            xg[c, rows(n_chip + i), :] = (value + sib_in[c, i].astype(f32)).astype(bf16)
            t_send(c, k).start()
            return carry

        lax.fori_loop(1, n_chip, chip_block, 0)
        value = jnp.dot(at_blk[rows(2 * chip + core), :], gg[c], preferred_element_type=f32)
        s_send(c, chip).wait_recv()
        own[c] = value + sib_in[c, chip].astype(f32)

        if c == 0:
            for k in range(1, n_col):
                z_arrival(other_col(k)).wait_recv()
            w_sum, b_sum = add_up(wz, n_col)
            wfin[me_r] = w_sum.astype(bf16)
            bg_ref[...] = b_sum
            for k in range(1, n_row):
                f_send(k).start()

    for c in range(n_chunk):
        total = own[c]
        for k in range(1, n_chip):
            src = other_chip(k)
            t_arrival(c, src).wait_recv()
            total = total + tot_in[c, src].astype(f32)
        fg_ref[:, pl.ds(c * width, width)] = total.astype(bf16)

    for k in range(1, n_row):
        f_arrival(other_row(k)).wait_recv()
    for r in range(n_row):
        wg_ref[pl.ds(r * w_rows, w_rows)] = wfin[r].astype(f32)

    for c in range(n_chunk):
        x_sib(c).wait_send()
        for k in range(1, n_chip):
            x_send(c, k).wait_send()
            t_send(c, k).wait_send()
        for k in range(1, n_col):
            p_send(c, k).wait_send()
            g_send(c, k).wait_send()
        for i in range(n_chip):
            s_send(c, i).wait_send()
    for k in range(1, n_row):
        w_send(k).wait_send()
        f_send(k).wait_send()
    for k in range(1, n_col):
        z_send(k).wait_send()


def per_device(n_row, n_col, node_features, tile_values, tile_rows, tile_cols, tile_count,
               weight, bias, cotangent):
    bf16, f32 = jnp.bfloat16, jnp.float32
    blocks = tile_values[0]
    slots, tile = blocks.shape[0], blocks.shape[-1]
    length, features = node_features.shape
    n_chunk = 2
    width = features // n_chunk
    n_chip = n_row // 2
    row_nodes, col_nodes = length * n_col, length * n_row
    row_tiles, col_tiles = row_nodes // tile, col_nodes // tile
    w_rows = features // n_row
    padded = w_rows + BIAS_ROWS

    slot_number = jnp.arange(slots, dtype=jnp.int32)
    place = jnp.where(slot_number < tile_count[0, 0],
                      tile_rows[0] * col_tiles + tile_cols[0], -1)
    hit = place[None, :] == jnp.arange(row_tiles * col_tiles, dtype=jnp.int32)[:, None]
    slot_map = jnp.min(jnp.where(hit, slot_number[None, :], slots), axis=1)

    dma = pltpu.SemaphoreType.DMA
    vmem = pl.BlockSpec(memory_space=pltpu.VMEM)
    anywhere = pl.BlockSpec(memory_space=pl.ANY)
    output, feature_grad, weight_sum, bias_sum = pl.pallas_call(
        functools.partial(layer_kernel, n_row, n_col, n_chunk),
        out_shape=(
            jax.ShapeDtypeStruct((length, features), bf16),
            jax.ShapeDtypeStruct((length, features), bf16),
            jax.ShapeDtypeStruct((features, features), f32),
            jax.ShapeDtypeStruct((1, features), f32),
        ),
        in_specs=[pl.BlockSpec(memory_space=pltpu.SMEM), anywhere, anywhere, anywhere, vmem, anywhere],
        out_specs=(vmem,) * 4,
        scratch_shapes=[
            pltpu.VMEM((slots + 1, tile, tile), bf16),
            pltpu.VMEM((row_nodes, col_nodes), bf16),
            pltpu.VMEM((col_nodes, row_nodes), bf16),
            pltpu.VMEM((features, features), bf16),
            pltpu.VMEM((length, features), bf16),
            pltpu.VMEM((n_chunk, col_nodes, width), bf16),
            pltpu.VMEM((n_chunk, row_nodes, width), bf16),
            pltpu.VMEM((n_chunk, n_col, length, width), bf16),
            pltpu.VMEM((n_chunk, length, width), f32),
            pltpu.VMEM((length, features), bf16),
            pltpu.VMEM((length, features), bf16),
            pltpu.VMEM((n_chunk, row_nodes, width), bf16),
            pltpu.VMEM((n_chunk, n_chip, length, width), bf16),
            pltpu.VMEM((n_chunk, n_chip, length, width), bf16),
            pltpu.VMEM((n_row, padded, features), bf16),
            pltpu.VMEM((n_row, padded, features), bf16),
            pltpu.VMEM((n_col, padded, features), bf16),
            pltpu.VMEM((n_row, w_rows, features), bf16),
            dma((3,)),
            dma((n_chunk,)),
            dma((n_chunk, n_chip)),
            dma((n_chunk, n_chip)),
            dma((n_chunk, n_row)),
            dma((n_chunk, n_col)),
            dma((n_chunk, n_col)),
            dma((n_chunk, n_col)),
            dma((n_chunk, n_col)),
            dma((n_chunk, n_chip)),
            dma((n_chunk, n_chip)),
            dma((n_chunk, n_chip)),
            dma((n_chunk, n_chip)),
            dma((n_row,)),
            dma((n_row,)),
            dma((n_col,)),
            dma((n_col,)),
            dma((n_row,)),
            dma((n_row,)),
        ],
        compiler_params=pltpu.CompilerParams(
            collective_id=0, has_side_effects=True, vmem_limit_bytes=62 * 1024 * 1024),
    )(slot_map, node_features, blocks, weight, bias[None, :], cotangent)
    grad_scale = 1.0 / math.sqrt(length * n_row * n_col)
    return output, feature_grad, weight_sum * grad_scale, bias_sum[0] * grad_scale


def solution(mesh):
    return jax.shard_map(
        functools.partial(per_device, mesh.shape["row"], mesh.shape["col"]),
        mesh=mesh,
        in_specs=(
            P(("col", "row"), None),
            P("row", "col", None, None),
            P("row", "col"),
            P("row", "col"),
            P("row", "col"),
            P(),
            P(),
            P(("row", "col"), None),
        ),
        out_specs=(P(("row", "col"), None), P(("col", "row"), None), P(), P()),
        check_vma=False,
    )
```

```python
import functools
import math

import jax
import jax.numpy as jnp
from jax import lax
from jax.experimental import pallas as pl
from jax.experimental.pallas import tpu as pltpu
from jax.sharding import PartitionSpec as P

MESH = pl.DeviceIdType.MESH
BIAS_ROWS = 16


def layer_kernel(
    n_row, n_col, n_chunk,
    slot_ref, x_ref, tiles_hbm, w_hbm, bias_ref, ct_hbm,
    out_ref, fg_ref, wg_ref, bg_ref,
    tiles, a_blk, at_blk, w_ref, ct_ref, xg, part, part_in, own, agg_sum, agg, gp_ref, gg,
    sib_in, tot_in, wb_out, wb_in, wz, wfin,
    local_sem, xl_sem, xs_sem, xf_sem, xr_sem, ps_sem, pr_sem, gs_sem, gr_sem,
    ss_sem, sr_sem, ts_sem, tr_sem, ws_sem, wr_sem, zs_sem, zr_sem, fs_sem, fr_sem,
):
    f32, bf16 = jnp.float32, jnp.bfloat16
    tile_slots = tiles_hbm.shape[0]
    tile = tiles_hbm.shape[1]
    length, features = x_ref.shape
    width = features // n_chunk
    row_tiles = length * n_col // tile
    col_tiles = length * n_row // tile
    n_chip = n_row // 2
    w_rows = features // n_row
    scale = 1.0 / math.sqrt(length * n_row * n_col)

    me_r, me_c = lax.axis_index("row"), lax.axis_index("col")
    chip, core = me_r // 2, me_r % 2
    sib = me_r + 1 - 2 * core

    def rows(i):
        return pl.ds(pl.multiple_of(i * length, length), length)

    def remote(src, dst, send, recv, **where):
        return pltpu.make_async_remote_copy(
            src_ref=src, dst_ref=dst, send_sem=send, recv_sem=recv,
            device_id=where, device_id_type=MESH,
        )

    def other_chip(k):
        return lax.rem(chip + k, n_chip)

    def other_col(k):
        return lax.rem(me_c + k, n_col)

    def other_row(k):
        return lax.rem(me_r + k, n_row)

    tiles_copy = pltpu.make_async_copy(tiles_hbm, tiles.at[pl.ds(0, tile_slots)], local_sem.at[0])
    w_copy = pltpu.make_async_copy(w_hbm, w_ref, local_sem.at[1])
    ct_copy = pltpu.make_async_copy(ct_hbm, ct_ref, local_sem.at[2])
    tiles_copy.start()

    def x_chunk(c):
        return x_ref.at[:, pl.ds(c * width, width)]

    def x_local(c):
        return pltpu.make_async_copy(x_chunk(c), xg.at[c, rows(me_r)], xl_sem.at[c])

    for c in range(n_chunk):
        x_local(c).start()
    w_copy.start()
    ct_copy.start()

    barrier = pltpu.get_barrier_semaphore()
    for k in range(1, n_row):
        pl.semaphore_signal(barrier, inc=1, device_id={"row": other_row(k)}, device_id_type=MESH)
    for k in range(1, n_col):
        pl.semaphore_signal(barrier, inc=1, device_id={"col": other_col(k)}, device_id_type=MESH)
    pl.semaphore_wait(barrier, n_row + n_col - 2)

    def x_send(c, k):
        return remote(x_chunk(c), xg.at[c, rows(me_r)], xs_sem.at[c, k], xr_sem.at[c, me_r],
                      row=2 * other_chip(k) + core)

    def x_sib(c):
        return remote(x_chunk(c), xg.at[c, rows(me_r)], xs_sem.at[c, 0], xr_sem.at[c, me_r], row=sib)

    def x_forward(c, k):
        src = 2 * other_chip(n_chip - k) + core
        block = xg.at[c, rows(src)]
        return remote(block, block, xf_sem.at[c, k - 1], xr_sem.at[c, src], row=sib)

    def x_arrival(c, src):
        block = xg.at[c, rows(src)]
        return remote(block, block, xf_sem.at[c, 0], xr_sem.at[c, src], row=sib)

    for c in range(n_chunk):
        for k in range(1, n_chip):
            x_send(c, k).start()
        x_sib(c).start()

    tiles[tile_slots] = jnp.zeros((tile, tile), bf16)
    tiles_copy.wait()

    def dense_row(i, carry):
        for j in range(col_tiles):
            value = tiles[slot_ref[i * col_tiles + j]]
            a_blk[pl.ds(pl.multiple_of(i * tile, tile), tile), pl.ds(j * tile, tile)] = value
        return carry

    lax.fori_loop(0, row_tiles, dense_row, 0)

    flip = (me_c >= n_col // 2).astype(jnp.int32)

    def mirrored(i):
        return i + flip * (n_col - 1 - 2 * i)

    place = mirrored(me_c)

    def p_send(c, dest):
        up = (dest > me_c).astype(jnp.int32)
        slot = jnp.where(dest == me_c - 1, n_col, dest)
        return remote(part.at[c, rows(dest)], part_in.at[c, slot], ps_sem.at[c, dest],
                      pr_sem.at[c, slot], col=me_c + 2 * up - 1)

    def p_arrival(c, slot):
        block = part_in.at[c, slot]
        return remote(block, block, ps_sem.at[c, 0], pr_sem.at[c, slot], col=other_col(1))

    def pass_on(c, dest, first):
        value = jnp.dot(a_blk[rows(dest), :], xg[c], preferred_element_type=f32)

        @pl.when(first)
        def _():
            part[c, rows(dest), :] = value.astype(bf16)

        @pl.when(jnp.logical_not(first))
        def _():
            p_arrival(c, dest).wait_recv()
            part[c, rows(dest), :] = (value + part_in[c, dest].astype(f32)).astype(bf16)

        p_send(c, dest).start()

    for c in range(n_chunk):
        x_local(c).wait()
        for k in range(1, n_chip):
            x_arrival(c, 2 * other_chip(n_chip - k) + core).wait_recv()
            x_forward(c, k).start()
        x_arrival(c, sib).wait_recv()
        for k in range(1, n_chip):
            x_arrival(c, 2 * other_chip(n_chip - k) + 1 - core).wait_recv()

        def forward_block(k, carry):
            @pl.when(n_col - k > place)
            def _():
                pass_on(c, mirrored(n_col - k), place == 0)

            @pl.when(k - 1 < place)
            def _():
                pass_on(c, mirrored(k - 1), place == n_col - 1)

            return carry

        lax.fori_loop(1, n_col, forward_block, 0)
        own[c] = jnp.dot(a_blk[rows(me_c), :], xg[c], preferred_element_type=f32)

    def dense_col(j, carry):
        for i in range(row_tiles):
            value = tiles[slot_ref[i * col_tiles + j]]
            at_blk[pl.ds(pl.multiple_of(j * tile, tile), tile), pl.ds(i * tile, tile)] = value.T
        return carry

    lax.fori_loop(0, col_tiles, dense_col, 0)

    w_copy.wait()
    ct_copy.wait()
    for c in range(n_chunk):
        agg_sum[...] = own[c]

        @pl.when(me_c > 0)
        def _():
            p_arrival(c, me_c).wait_recv()
            agg_sum[...] += part_in[c, me_c].astype(f32)

        @pl.when(me_c < n_col - 1)
        def _():
            p_arrival(c, n_col).wait_recv()
            agg_sum[...] += part_in[c, n_col].astype(f32)

        total = agg_sum[...]
        agg[:, pl.ds(c * width, width)] = total.astype(bf16)

    pre = jnp.dot(agg[...], w_ref[...], preferred_element_type=f32) + bias_ref[...]
    sig = jax.nn.sigmoid(pre)
    grad_pre = (ct_ref[...].astype(f32) * sig * (1.0 + pre * (1.0 - sig))).astype(bf16)
    gp_ref[...] = grad_pre
    out_ref[...] = (pre * sig).astype(bf16)

    def g_send(c, src, step):
        block = gg.at[c, rows(src)]
        slot = jnp.where((src == me_c) & (step < 0), n_col, src)
        return remote(block, block, gs_sem.at[c, slot], gr_sem.at[c, src], col=me_c + step)

    def g_arrival(c, src):
        block = gg.at[c, rows(src)]
        return remote(block, block, gs_sem.at[c, 0], gr_sem.at[c, src], col=other_col(1))

    has_right, has_left = me_c < n_col - 1, me_c > 0

    def g_own(c, act):
        @pl.when(has_right)
        def _():
            act(g_send(c, me_c, 1))

        @pl.when(has_left)
        def _():
            act(g_send(c, me_c, -1))

    def start(copy):
        copy.start()

    def sent(copy):
        copy.wait_send()

    def g_from(c, k, arrive, act):
        @pl.when(me_c - k >= 0)
        def _():
            if arrive:
                g_arrival(c, me_c - k).wait_recv()

            @pl.when(has_right)
            def _():
                act(g_send(c, me_c - k, 1))

        @pl.when(me_c + k < n_col)
        def _():
            if arrive:
                g_arrival(c, me_c + k).wait_recv()

            @pl.when(has_left)
            def _():
                act(g_send(c, me_c + k, -1))

    for c in range(n_chunk):
        gg[c, rows(me_c), :] = lax.dot_general(
            gp_ref[...], w_ref[pl.ds(c * width, width), :], (((1,), (1,)), ((), ())),
            preferred_element_type=f32).astype(bf16)
        if c == 0:
            g_own(c, start)

    bias_sum = jnp.sum(gp_ref[...].astype(f32), axis=0, keepdims=True)

    def bias_rows(value):
        high = value.astype(bf16).astype(f32)
        low = value - high
        index = lax.broadcasted_iota(jnp.int32, (BIAS_ROWS, features), 0)
        block = jnp.where(index == 0, high, jnp.where(index == 1, low, 0.0))
        return block.astype(bf16)

    bias_block = bias_rows(bias_sum)
    w_local = lax.dot_general(agg[...], gp_ref[...], (((0,), (0,)), ((), ())),
                              preferred_element_type=f32)
    for r in range(n_row):
        wb_out[r, pl.ds(0, w_rows)] = w_local[r * w_rows:(r + 1) * w_rows].astype(bf16)
        wb_out[r, pl.ds(w_rows, BIAS_ROWS)] = bias_block

    def w_send(k):
        dest = other_row(k)
        return remote(wb_out.at[dest], wb_in.at[me_r], ws_sem.at[k - 1], wr_sem.at[me_r], row=dest)

    def w_arrival(src):
        return remote(wb_in.at[src], wb_in.at[src], ws_sem.at[0], wr_sem.at[src], row=src)

    for k in range(1, n_row):
        w_send(k).start()
    wb_in[me_r] = wb_out[me_r]
    def add_up(ref, count):
        total = ref[0].astype(f32)
        for i in range(1, count):
            total = total + ref[i].astype(f32)
        return total[:w_rows], total[w_rows:w_rows + 1] + total[w_rows + 1:w_rows + 2]

    root = n_col // 2

    def store_term(ref, index, value):
        w_part, b_part = value
        ref[index, pl.ds(0, w_rows)] = w_part.astype(bf16)
        ref[index, pl.ds(w_rows, BIAS_ROWS)] = bias_rows(b_part)

    def z_send():
        return remote(wz.at[me_c], wz.at[me_c], zs_sem.at[n_col], zr_sem.at[me_c], col=root)

    def z_arrival(src):
        return remote(wz.at[src], wz.at[src], zs_sem.at[0], zr_sem.at[src], col=src)

    def z_back(dest):
        return remote(wz.at[n_col], wz.at[n_col], zs_sem.at[dest], zr_sem.at[n_col], col=dest)

    def others_of_root(act):
        for i in range(n_col):
            if i != root:
                act(i)

    def reduce_rows():
        for k in range(1, n_row):
            w_arrival(other_row(k)).wait_recv()
        store_term(wz, me_c, add_up(wb_in, n_row))

        @pl.when(me_c != root)
        def _():
            z_send().start()

    def reduce_cols():
        @pl.when(me_c == root)
        def _():
            others_of_root(lambda i: z_arrival(i).wait_recv())
            store_term(wz, n_col, add_up(wz, n_col))
            others_of_root(lambda i: z_back(i).start())

    def gather_rows():
        @pl.when(me_c != root)
        def _():
            z_back(other_col(1)).wait_recv()

        wfin[me_r] = wz[n_col, pl.ds(0, w_rows)]
        last = wz[n_col, pl.ds(w_rows, BIAS_ROWS)].astype(f32)
        bg_ref[...] = (last[0:1] + last[1:2]) * scale
        for k in range(1, n_row):
            f_send(k).start()

    def s_send(c, i):
        return remote(xg.at[c, rows(i)], sib_in.at[c, i], ss_sem.at[c, i], sr_sem.at[c, i], row=sib)

    def t_send(c, k):
        dest = other_chip(k)
        return remote(xg.at[c, rows(n_chip + dest)], tot_in.at[c, chip], ts_sem.at[c, k - 1],
                      tr_sem.at[c, chip], row=2 * dest + core)

    def t_arrival(c, src):
        block = tot_in.at[c, src]
        return remote(block, block, ts_sem.at[c, 0], tr_sem.at[c, src], row=2 * src + core)

    def f_send(k):
        block = wfin.at[me_r]
        return remote(block, block, fs_sem.at[k - 1], fr_sem.at[me_r], row=other_row(k))

    def f_arrival(src):
        return remote(wfin.at[src], wfin.at[src], fs_sem.at[0], fr_sem.at[src], row=src)

    for c in range(n_chunk):
        for k in range(1, n_chip):
            x_forward(c, k).wait_send()

    def sibling_blocks(c):
        def one(k, carry):
            i = other_chip(k)
            xg[c, rows(i), :] = jnp.dot(at_blk[rows(2 * i + 1 - core), :], gg[c],
                                        preferred_element_type=f32).astype(bf16)
            s_send(c, i).start()
            return carry

        lax.fori_loop(1, n_chip + 1, one, 0)

    def chip_blocks(c):
        def one(k, carry):
            i = other_chip(k)
            value = jnp.dot(at_blk[rows(2 * i + core), :], gg[c], preferred_element_type=f32)
            s_send(c, i).wait_recv()
            xg[c, rows(n_chip + i), :] = (value + sib_in[c, i].astype(f32)).astype(bf16)
            t_send(c, k).start()
            return carry

        lax.fori_loop(1, n_chip, one, 0)
        value = jnp.dot(at_blk[rows(2 * chip + core), :], gg[c], preferred_element_type=f32)
        s_send(c, chip).wait_recv()
        own[c] = value + sib_in[c, chip].astype(f32)

    for c in range(n_chunk):
        for k in range(1 if c == 0 else 2, n_col):
            g_from(c, k, True, start)
            if k == 1 and n_chunk > 1:
                g_own(1, start)
        if c == 0:
            reduce_rows()
        if c == n_chunk - 1:
            gather_rows()
        sibling_blocks(c)
        if c + 1 < n_chunk:
            g_from(c + 1, 1, True, start)
            if c + 2 < n_chunk:
                g_own(c + 2, start)
        chip_blocks(c)
        if c == 0:
            reduce_cols()

    for c in range(n_chunk):
        total = own[c]
        for k in range(1, n_chip):
            src = other_chip(k)
            t_arrival(c, src).wait_recv()
            total = total + tot_in[c, src].astype(f32)
        fg_ref[:, pl.ds(c * width, width)] = total.astype(bf16)

    for k in range(1, n_row):
        f_arrival(other_row(k)).wait_recv()
    for r in range(n_row):
        wg_ref[pl.ds(r * w_rows, w_rows)] = wfin[r].astype(f32) * scale

    for c in range(n_chunk):
        x_sib(c).wait_send()
        for k in range(1, n_chip):
            x_send(c, k).wait_send()
            t_send(c, k).wait_send()
        for k in range(1, n_col):
            p_send(c, other_col(k)).wait_send()
            g_from(c, k, False, sent)
        g_own(c, sent)
        for i in range(n_chip):
            s_send(c, i).wait_send()
    for k in range(1, n_row):
        w_send(k).wait_send()
        f_send(k).wait_send()

    @pl.when(me_c != root)
    def _():
        z_send().wait_send()

    @pl.when(me_c == root)
    def _():
        others_of_root(lambda i: z_back(i).wait_send())


def per_device(n_row, n_col, node_features, tile_values, tile_rows, tile_cols, tile_count,
               weight, bias, cotangent):
    bf16, f32 = jnp.bfloat16, jnp.float32
    blocks = tile_values[0]
    slots, tile = blocks.shape[0], blocks.shape[-1]
    length, features = node_features.shape
    n_chunk = 2
    width = features // n_chunk
    n_chip = n_row // 2
    row_nodes, col_nodes = length * n_col, length * n_row
    row_tiles, col_tiles = row_nodes // tile, col_nodes // tile
    w_rows = features // n_row
    padded = w_rows + BIAS_ROWS

    slot_number = jnp.arange(slots, dtype=jnp.int32)
    place = jnp.where(slot_number < tile_count[0, 0],
                      tile_rows[0] * col_tiles + tile_cols[0], -1)
    hit = place[None, :] == jnp.arange(row_tiles * col_tiles, dtype=jnp.int32)[:, None]
    slot_map = jnp.min(jnp.where(hit, slot_number[None, :], slots), axis=1)

    dma = pltpu.SemaphoreType.DMA
    vmem = pl.BlockSpec(memory_space=pltpu.VMEM)
    anywhere = pl.BlockSpec(memory_space=pl.ANY)
    output, feature_grad, weight_grad, bias_grad = pl.pallas_call(
        functools.partial(layer_kernel, n_row, n_col, n_chunk),
        out_shape=(
            jax.ShapeDtypeStruct((length, features), bf16),
            jax.ShapeDtypeStruct((length, features), bf16),
            jax.ShapeDtypeStruct((features, features), f32),
            jax.ShapeDtypeStruct((1, features), f32),
        ),
        in_specs=[pl.BlockSpec(memory_space=pltpu.SMEM), anywhere, anywhere, anywhere, vmem, anywhere],
        out_specs=(vmem,) * 4,
        scratch_shapes=[
            pltpu.VMEM((slots + 1, tile, tile), bf16),
            pltpu.VMEM((row_nodes, col_nodes), bf16),
            pltpu.VMEM((col_nodes, row_nodes), bf16),
            pltpu.VMEM((features, features), bf16),
            pltpu.VMEM((length, features), bf16),
            pltpu.VMEM((n_chunk, col_nodes, width), bf16),
            pltpu.VMEM((n_chunk, row_nodes, width), bf16),
            pltpu.VMEM((n_chunk, n_col + 1, length, width), bf16),
            pltpu.VMEM((n_chunk, length, width), f32),
            pltpu.VMEM((length, width), f32),
            pltpu.VMEM((length, features), bf16),
            pltpu.VMEM((length, features), bf16),
            pltpu.VMEM((n_chunk, row_nodes, width), bf16),
            pltpu.VMEM((n_chunk, n_chip, length, width), bf16),
            pltpu.VMEM((n_chunk, n_chip, length, width), bf16),
            pltpu.VMEM((n_row, padded, features), bf16),
            pltpu.VMEM((n_row, padded, features), bf16),
            pltpu.VMEM((n_col + 1, padded, features), bf16),
            pltpu.VMEM((n_row, w_rows, features), bf16),
            dma((3,)),
            dma((n_chunk,)),
            dma((n_chunk, n_chip)),
            dma((n_chunk, n_chip)),
            dma((n_chunk, n_row)),
            dma((n_chunk, n_col + 1)),
            dma((n_chunk, n_col + 1)),
            dma((n_chunk, n_col + 1)),
            dma((n_chunk, n_col + 1)),
            dma((n_chunk, n_chip)),
            dma((n_chunk, n_chip)),
            dma((n_chunk, n_chip)),
            dma((n_chunk, n_chip)),
            dma((n_row,)),
            dma((n_row,)),
            dma((n_col + 1,)),
            dma((n_col + 1,)),
            dma((n_row,)),
            dma((n_row,)),
        ],
        compiler_params=pltpu.CompilerParams(
            collective_id=0, has_side_effects=True, vmem_limit_bytes=62 * 1024 * 1024),
    )(slot_map, node_features, blocks, weight, bias[None, :], cotangent)
    return output, feature_grad, weight_grad, bias_grad[0]


def solution(mesh):
    return jax.shard_map(
        functools.partial(per_device, mesh.shape["row"], mesh.shape["col"]),
        mesh=mesh,
        in_specs=(
            P(("col", "row"), None),
            P("row", "col", None, None),
            P("row", "col"),
            P("row", "col"),
            P("row", "col"),
            P(),
            P(),
            P(("row", "col"), None),
        ),
        out_specs=(P(("row", "col"), None), P(("col", "row"), None), P(), P()),
        check_vma=False,
    )
```

```python
import functools
import math

import jax
import jax.numpy as jnp
from jax import lax
from jax.experimental import pallas as pl
from jax.experimental.pallas import tpu as pltpu
from jax.sharding import PartitionSpec as P

MESH = pl.DeviceIdType.MESH
BIAS_ROWS = 16


def layer_kernel(
    n_row, n_col, n_chunk,
    slot_ref, x_ref, tiles_hbm, w_hbm, bias_ref, ct_hbm,
    out_ref, fg_ref, wg_ref, bg_ref,
    tiles, a_blk, at_blk, w_ref, ct_ref, xg, part, part_in, own, agg_sum, agg, gp_ref, gg,
    sib_in, tot_in, wb_out, wb_in, wz, wfin,
    local_sem, xl_sem, xs_sem, xf_sem, xr_sem, ps_sem, pr_sem, gs_sem, gr_sem,
    ss_sem, sr_sem, ts_sem, tr_sem, ws_sem, wr_sem, zs_sem, zr_sem, fs_sem, fr_sem,
):
    f32, bf16 = jnp.float32, jnp.bfloat16
    tile_slots = tiles_hbm.shape[0]
    tile = tiles_hbm.shape[1]
    length, features = x_ref.shape
    width = features // n_chunk
    row_tiles = length * n_col // tile
    col_tiles = length * n_row // tile
    n_chip = n_row // 2
    w_rows = features // n_row
    scale = 1.0 / math.sqrt(length * n_row * n_col)

    me_r, me_c = lax.axis_index("row"), lax.axis_index("col")
    chip, core = me_r // 2, me_r % 2
    sib = me_r + 1 - 2 * core

    def rows(i):
        return pl.ds(pl.multiple_of(i * length, length), length)

    def remote(src, dst, send, recv, **where):
        return pltpu.make_async_remote_copy(
            src_ref=src, dst_ref=dst, send_sem=send, recv_sem=recv,
            device_id=where, device_id_type=MESH,
        )

    def other_chip(k):
        return lax.rem(chip + k, n_chip)

    def other_col(k):
        return lax.rem(me_c + k, n_col)

    def other_row(k):
        return lax.rem(me_r + k, n_row)

    tiles_copy = pltpu.make_async_copy(tiles_hbm, tiles.at[pl.ds(0, tile_slots)], local_sem.at[0])
    w_copy = pltpu.make_async_copy(w_hbm, w_ref, local_sem.at[1])
    ct_copy = pltpu.make_async_copy(ct_hbm, ct_ref, local_sem.at[2])
    tiles_copy.start()

    def x_chunk(c):
        return x_ref.at[:, pl.ds(c * width, width)]

    def x_local(c):
        return pltpu.make_async_copy(x_chunk(c), xg.at[c, rows(me_r)], xl_sem.at[c])

    for c in range(n_chunk):
        x_local(c).start()
    w_copy.start()
    ct_copy.start()

    barrier = pltpu.get_barrier_semaphore()
    for k in range(1, n_row):
        pl.semaphore_signal(barrier, inc=1, device_id={"row": other_row(k)}, device_id_type=MESH)
    for k in range(1, n_col):
        pl.semaphore_signal(barrier, inc=1, device_id={"col": other_col(k)}, device_id_type=MESH)
    pl.semaphore_wait(barrier, n_row + n_col - 2)

    def x_send(c, k):
        return remote(x_chunk(c), xg.at[c, rows(me_r)], xs_sem.at[c, k], xr_sem.at[c, me_r],
                      row=2 * other_chip(k) + core)

    def x_sib(c):
        return remote(x_chunk(c), xg.at[c, rows(me_r)], xs_sem.at[c, 0], xr_sem.at[c, me_r], row=sib)

    def x_forward(c, k):
        src = 2 * other_chip(n_chip - k) + core
        block = xg.at[c, rows(src)]
        return remote(block, block, xf_sem.at[c, k - 1], xr_sem.at[c, src], row=sib)

    def x_arrival(c, src):
        block = xg.at[c, rows(src)]
        return remote(block, block, xf_sem.at[c, 0], xr_sem.at[c, src], row=sib)

    for c in range(n_chunk):
        for k in range(1, n_chip):
            x_send(c, k).start()
        x_sib(c).start()

    tiles[tile_slots] = jnp.zeros((tile, tile), bf16)
    tiles_copy.wait()

    def dense_row(i, carry):
        for j in range(col_tiles):
            value = tiles[slot_ref[i * col_tiles + j]]
            a_blk[pl.ds(pl.multiple_of(i * tile, tile), tile), pl.ds(j * tile, tile)] = value
        return carry

    lax.fori_loop(0, row_tiles, dense_row, 0)

    flip = (me_c >= n_col // 2).astype(jnp.int32)

    def mirrored(i):
        return i + flip * (n_col - 1 - 2 * i)

    place = mirrored(me_c)

    def p_send(c, dest):
        up = (dest > me_c).astype(jnp.int32)
        slot = jnp.where(dest == me_c - 1, n_col, dest)
        return remote(part.at[c, rows(dest)], part_in.at[c, slot], ps_sem.at[c, dest],
                      pr_sem.at[c, slot], col=me_c + 2 * up - 1)

    def p_arrival(c, slot):
        block = part_in.at[c, slot]
        return remote(block, block, ps_sem.at[c, 0], pr_sem.at[c, slot], col=other_col(1))

    def pass_on(c, dest, first):
        value = jnp.dot(a_blk[rows(dest), :], xg[c], preferred_element_type=f32)

        @pl.when(first)
        def _():
            part[c, rows(dest), :] = value.astype(bf16)

        @pl.when(jnp.logical_not(first))
        def _():
            p_arrival(c, dest).wait_recv()
            part[c, rows(dest), :] = (value + part_in[c, dest].astype(f32)).astype(bf16)

        p_send(c, dest).start()

    for c in range(n_chunk):
        x_local(c).wait()
        for k in range(1, n_chip):
            x_arrival(c, 2 * other_chip(n_chip - k) + core).wait_recv()
            x_forward(c, k).start()
        x_arrival(c, sib).wait_recv()
        for k in range(1, n_chip):
            x_arrival(c, 2 * other_chip(n_chip - k) + 1 - core).wait_recv()

        def forward_block(k, carry):
            @pl.when(n_col - k > place)
            def _():
                pass_on(c, mirrored(n_col - k), place == 0)

            @pl.when(k - 1 < place)
            def _():
                pass_on(c, mirrored(k - 1), place == n_col - 1)

            return carry

        lax.fori_loop(1, n_col, forward_block, 0)
        own[c] = jnp.dot(a_blk[rows(me_c), :], xg[c], preferred_element_type=f32)

    def dense_col(j, carry):
        for i in range(row_tiles):
            value = tiles[slot_ref[i * col_tiles + j]]
            at_blk[pl.ds(pl.multiple_of(j * tile, tile), tile), pl.ds(i * tile, tile)] = value.T
        return carry

    lax.fori_loop(0, col_tiles, dense_col, 0)

    w_copy.wait()
    ct_copy.wait()
    for c in range(n_chunk):
        agg_sum[...] = own[c]

        @pl.when(me_c > 0)
        def _():
            p_arrival(c, me_c).wait_recv()
            agg_sum[...] += part_in[c, me_c].astype(f32)

        @pl.when(me_c < n_col - 1)
        def _():
            p_arrival(c, n_col).wait_recv()
            agg_sum[...] += part_in[c, n_col].astype(f32)

        total = agg_sum[...]
        agg[:, pl.ds(c * width, width)] = total.astype(bf16)

    pre = jnp.dot(agg[...], w_ref[...], preferred_element_type=f32) + bias_ref[...]
    sig = jax.nn.sigmoid(pre)
    grad_pre = (ct_ref[...].astype(f32) * sig * (1.0 + pre * (1.0 - sig))).astype(bf16)
    gp_ref[...] = grad_pre
    out_ref[...] = (pre * sig).astype(bf16)

    def g_send(c, src, step):
        block = gg.at[c, rows(src)]
        slot = jnp.where((src == me_c) & (step < 0), n_col, src)
        return remote(block, block, gs_sem.at[c, slot], gr_sem.at[c, src], col=me_c + step)

    def g_arrival(c, src):
        block = gg.at[c, rows(src)]
        return remote(block, block, gs_sem.at[c, 0], gr_sem.at[c, src], col=other_col(1))

    has_right, has_left = me_c < n_col - 1, me_c > 0

    def g_own(c, act):
        @pl.when(has_right)
        def _():
            act(g_send(c, me_c, 1))

        @pl.when(has_left)
        def _():
            act(g_send(c, me_c, -1))

    def start(copy):
        copy.start()

    def sent(copy):
        copy.wait_send()

    def g_from(c, k, arrive, act):
        @pl.when(me_c - k >= 0)
        def _():
            if arrive:
                g_arrival(c, me_c - k).wait_recv()

            @pl.when(has_right)
            def _():
                act(g_send(c, me_c - k, 1))

        @pl.when(me_c + k < n_col)
        def _():
            if arrive:
                g_arrival(c, me_c + k).wait_recv()

            @pl.when(has_left)
            def _():
                act(g_send(c, me_c + k, -1))

    for c in range(n_chunk):
        gg[c, rows(me_c), :] = lax.dot_general(
            gp_ref[...], w_ref[pl.ds(c * width, width), :], (((1,), (1,)), ((), ())),
            preferred_element_type=f32).astype(bf16)
        if c == 0:
            g_own(c, start)

    bias_sum = jnp.sum(gp_ref[...].astype(f32), axis=0, keepdims=True)

    def bias_rows(value):
        high = value.astype(bf16).astype(f32)
        low = value - high
        index = lax.broadcasted_iota(jnp.int32, (BIAS_ROWS, features), 0)
        block = jnp.where(index == 0, high, jnp.where(index == 1, low, 0.0))
        return block.astype(bf16)

    bias_block = bias_rows(bias_sum)
    w_local = lax.dot_general(agg[...], gp_ref[...], (((0,), (0,)), ((), ())),
                              preferred_element_type=f32)
    for r in range(n_row):
        wb_out[r, pl.ds(0, w_rows)] = w_local[r * w_rows:(r + 1) * w_rows].astype(bf16)
        wb_out[r, pl.ds(w_rows, BIAS_ROWS)] = bias_block

    def w_send(k):
        dest = other_row(k)
        return remote(wb_out.at[dest], wb_in.at[me_r], ws_sem.at[k - 1], wr_sem.at[me_r], row=dest)

    def w_arrival(src):
        return remote(wb_in.at[src], wb_in.at[src], ws_sem.at[0], wr_sem.at[src], row=src)

    for k in range(1, n_row):
        w_send(k).start()
    wb_in[me_r] = wb_out[me_r]
    def add_up(ref, count):
        total = ref[0].astype(f32)
        for i in range(1, count):
            total = total + ref[i].astype(f32)
        return total[:w_rows], total[w_rows:w_rows + 1] + total[w_rows + 1:w_rows + 2]

    root = n_col // 2

    def store_term(ref, index, value):
        w_part, b_part = value
        ref[index, pl.ds(0, w_rows)] = w_part.astype(bf16)
        ref[index, pl.ds(w_rows, BIAS_ROWS)] = bias_rows(b_part)

    def z_send():
        return remote(wz.at[me_c], wz.at[me_c], zs_sem.at[n_col], zr_sem.at[me_c], col=root)

    def z_arrival(src):
        return remote(wz.at[src], wz.at[src], zs_sem.at[0], zr_sem.at[src], col=src)

    def z_back(dest):
        return remote(wz.at[n_col], wz.at[n_col], zs_sem.at[dest], zr_sem.at[n_col], col=dest)

    def others_of_root(act):
        for i in range(n_col):
            if i != root:
                act(i)

    def reduce_rows():
        for k in range(1, n_row):
            w_arrival(other_row(k)).wait_recv()
        store_term(wz, me_c, add_up(wb_in, n_row))

        @pl.when(me_c != root)
        def _():
            z_send().start()

    def reduce_cols():
        @pl.when(me_c == root)
        def _():
            others_of_root(lambda i: z_arrival(i).wait_recv())
            store_term(wz, n_col, add_up(wz, n_col))
            others_of_root(lambda i: z_back(i).start())

    def gather_rows():
        @pl.when(me_c != root)
        def _():
            z_back(other_col(1)).wait_recv()

        wfin[me_r] = wz[n_col, pl.ds(0, w_rows)]
        last = wz[n_col, pl.ds(w_rows, BIAS_ROWS)].astype(f32)
        bg_ref[...] = (last[0:1] + last[1:2]) * scale
        for k in range(1, n_row):
            f_send(k).start()

    def s_send(c, i):
        return remote(xg.at[c, rows(i)], sib_in.at[c, i], ss_sem.at[c, i], sr_sem.at[c, i], row=sib)

    def t_send(c, k):
        dest = other_chip(k)
        return remote(xg.at[c, rows(n_chip + dest)], tot_in.at[c, chip], ts_sem.at[c, k - 1],
                      tr_sem.at[c, chip], row=2 * dest + core)

    def t_arrival(c, src):
        block = tot_in.at[c, src]
        return remote(block, block, ts_sem.at[c, 0], tr_sem.at[c, src], row=2 * src + core)

    def f_send(k):
        block = wfin.at[me_r]
        return remote(block, block, fs_sem.at[k - 1], fr_sem.at[me_r], row=other_row(k))

    def f_arrival(src):
        return remote(wfin.at[src], wfin.at[src], fs_sem.at[0], fr_sem.at[src], row=src)

    for c in range(n_chunk):
        for k in range(1, n_chip):
            x_forward(c, k).wait_send()

    def sibling_blocks(c):
        def one(k, carry):
            i = other_chip(k)
            xg[c, rows(i), :] = jnp.dot(at_blk[rows(2 * i + 1 - core), :], gg[c],
                                        preferred_element_type=f32).astype(bf16)
            s_send(c, i).start()
            return carry

        lax.fori_loop(1, n_chip + 1, one, 0)

    def chip_blocks(c):
        def one(k, carry):
            i = other_chip(k)
            value = jnp.dot(at_blk[rows(2 * i + core), :], gg[c], preferred_element_type=f32)
            s_send(c, i).wait_recv()
            xg[c, rows(n_chip + i), :] = (value + sib_in[c, i].astype(f32)).astype(bf16)
            t_send(c, k).start()
            return carry

        lax.fori_loop(1, n_chip, one, 0)
        value = jnp.dot(at_blk[rows(2 * chip + core), :], gg[c], preferred_element_type=f32)
        s_send(c, chip).wait_recv()
        own[c] = value + sib_in[c, chip].astype(f32)

    for c in range(n_chunk):
        for k in range(1 if c == 0 else 2, n_col):
            g_from(c, k, True, start)
            if k == 1 and n_chunk > 1:
                g_own(1, start)
        if c == 1:
            reduce_rows()
        if c == n_chunk - 1:
            gather_rows()
        sibling_blocks(c)
        if c + 1 < n_chunk:
            g_from(c + 1, 1, True, start)
            if c + 2 < n_chunk:
                g_own(c + 2, start)
        if c == n_chunk - 2:
            reduce_cols()
        chip_blocks(c)

    for c in range(n_chunk):
        total = own[c]
        for k in range(1, n_chip):
            src = other_chip(k)
            t_arrival(c, src).wait_recv()
            total = total + tot_in[c, src].astype(f32)
        fg_ref[:, pl.ds(c * width, width)] = total.astype(bf16)

    for k in range(1, n_row):
        f_arrival(other_row(k)).wait_recv()
    for r in range(n_row):
        wg_ref[pl.ds(r * w_rows, w_rows)] = wfin[r].astype(f32) * scale

    for c in range(n_chunk):
        x_sib(c).wait_send()
        for k in range(1, n_chip):
            x_send(c, k).wait_send()
            t_send(c, k).wait_send()
        for k in range(1, n_col):
            p_send(c, other_col(k)).wait_send()
            g_from(c, k, False, sent)
        g_own(c, sent)
        for i in range(n_chip):
            s_send(c, i).wait_send()
    for k in range(1, n_row):
        w_send(k).wait_send()
        f_send(k).wait_send()

    @pl.when(me_c != root)
    def _():
        z_send().wait_send()

    @pl.when(me_c == root)
    def _():
        others_of_root(lambda i: z_back(i).wait_send())


def copy_kernel(*refs):
    sems = refs[-1]
    count = (len(refs) - 1) // 2
    copies = [pltpu.make_async_copy(refs[i], refs[count + i], sems.at[i]) for i in range(count)]
    for copy in copies:
        copy.start()
    for copy in copies:
        copy.wait()


def per_device(n_row, n_col, node_features, tile_values, tile_rows, tile_cols, tile_count,
               weight, bias, cotangent):
    bf16, f32 = jnp.bfloat16, jnp.float32
    blocks = tile_values[0]
    slots, tile = blocks.shape[0], blocks.shape[-1]
    length, features = node_features.shape
    n_chunk = 4
    width = features // n_chunk
    n_chip = n_row // 2
    row_nodes, col_nodes = length * n_col, length * n_row
    row_tiles, col_tiles = row_nodes // tile, col_nodes // tile
    w_rows = features // n_row
    padded = w_rows + BIAS_ROWS

    slot_number = jnp.arange(slots, dtype=jnp.int32)
    place = jnp.where(slot_number < tile_count[0, 0],
                      tile_rows[0] * col_tiles + tile_cols[0], -1)
    hit = place[None, :] == jnp.arange(row_tiles * col_tiles, dtype=jnp.int32)[:, None]
    slot_map = jnp.min(jnp.where(hit, slot_number[None, :], slots), axis=1)

    dma = pltpu.SemaphoreType.DMA
    vmem = pl.BlockSpec(memory_space=pltpu.VMEM)
    anywhere = pl.BlockSpec(memory_space=pl.ANY)
    output, feature_grad, weight_grad, bias_grad = pl.pallas_call(
        functools.partial(layer_kernel, n_row, n_col, n_chunk),
        out_shape=(
            jax.ShapeDtypeStruct((length, features), bf16),
            jax.ShapeDtypeStruct((length, features), bf16),
            jax.ShapeDtypeStruct((features, features), f32),
            jax.ShapeDtypeStruct((1, features), f32),
        ),
        in_specs=[pl.BlockSpec(memory_space=pltpu.SMEM), anywhere, anywhere, anywhere, vmem, anywhere],
        out_specs=(vmem,) * 4,
        scratch_shapes=[
            pltpu.VMEM((slots + 1, tile, tile), bf16),
            pltpu.VMEM((row_nodes, col_nodes), bf16),
            pltpu.VMEM((col_nodes, row_nodes), bf16),
            pltpu.VMEM((features, features), bf16),
            pltpu.VMEM((length, features), bf16),
            pltpu.VMEM((n_chunk, col_nodes, width), bf16),
            pltpu.VMEM((n_chunk, row_nodes, width), bf16),
            pltpu.VMEM((n_chunk, n_col + 1, length, width), bf16),
            pltpu.VMEM((n_chunk, length, width), f32),
            pltpu.VMEM((length, width), f32),
            pltpu.VMEM((length, features), bf16),
            pltpu.VMEM((length, features), bf16),
            pltpu.VMEM((n_chunk, row_nodes, width), bf16),
            pltpu.VMEM((n_chunk, n_chip, length, width), bf16),
            pltpu.VMEM((n_chunk, n_chip, length, width), bf16),
            pltpu.VMEM((n_row, padded, features), bf16),
            pltpu.VMEM((n_row, padded, features), bf16),
            pltpu.VMEM((n_col + 1, padded, features), bf16),
            pltpu.VMEM((n_row, w_rows, features), bf16),
            dma((3,)),
            dma((n_chunk,)),
            dma((n_chunk, n_chip)),
            dma((n_chunk, n_chip)),
            dma((n_chunk, n_row)),
            dma((n_chunk, n_col + 1)),
            dma((n_chunk, n_col + 1)),
            dma((n_chunk, n_col + 1)),
            dma((n_chunk, n_col + 1)),
            dma((n_chunk, n_chip)),
            dma((n_chunk, n_chip)),
            dma((n_chunk, n_chip)),
            dma((n_chunk, n_chip)),
            dma((n_row,)),
            dma((n_row,)),
            dma((n_col + 1,)),
            dma((n_col + 1,)),
            dma((n_row,)),
            dma((n_row,)),
        ],
        compiler_params=pltpu.CompilerParams(
            collective_id=0, has_side_effects=True, vmem_limit_bytes=62 * 1024 * 1024),
    )(slot_map, node_features, blocks, weight, bias[None, :], cotangent)
    results = (output, feature_grad, weight_grad, bias_grad)
    output, feature_grad, weight_grad, bias_grad = pl.pallas_call(
        copy_kernel,
        out_shape=tuple(jax.ShapeDtypeStruct(r.shape, r.dtype) for r in results),
        in_specs=[anywhere] * len(results),
        out_specs=(anywhere,) * len(results),
        scratch_shapes=[dma((len(results),))],
        compiler_params=pltpu.CompilerParams(vmem_limit_bytes=62 * 1024 * 1024),
    )(*results)
    return output, feature_grad, weight_grad, bias_grad[0]


def solution(mesh):
    return jax.shard_map(
        functools.partial(per_device, mesh.shape["row"], mesh.shape["col"]),
        mesh=mesh,
        in_specs=(
            P(("col", "row"), None),
            P("row", "col", None, None),
            P("row", "col"),
            P("row", "col"),
            P("row", "col"),
            P(),
            P(),
            P(("row", "col"), None),
        ),
        out_specs=(P(("row", "col"), None), P(("col", "row"), None), P(), P()),
        check_vma=False,
    )
```
